32 devices in a mesh: row: 8 (over z, core), col: 4 (over y, x).
Axes of the slice: x: 2, y: 2, z: 4, core: 2. Of those that a mesh axis runs over, the one named last changes fastest.
Arguments:
- blocks: bfloat16 [256, 16, 128, 128], P('row', 'col'), may hold values from -0.8984375 to 0.8984375
- pattern: int32 [256, 16], replicated, may hold values from 0 to 255, as said below
- anchors: int32 [3, 256, 16], replicated, may hold values from 0 to 127, as said below
- basis_x: bfloat16 [16, 128], replicated, may hold values from -0.5 to 0.5
- basis_yz: bfloat16 [128, 256], replicated, may hold values from -0.5 to 0.5
Outputs:
- square: float32 [256, 16, 128, 128], P('row', 'col')
- grid_values: float32 [128, 128, 128], P('row', 'col')
The draws below stay inside these ranges and needn't reach their ends.
Inputs may be any that keep to these rules, and one draw needn't show every extreme that they name: pattern[i,k] = (i + d) mod 256 with -8 <= d <= 8; the 16 columns of a row are distinct. For block row i in group g = i // 32, anchors[0,i,k] = (g * 16 - 16 / 2 + u) mod 128 with 0 <= u <= 16; anchors[1,i,k] <= 112; anchors[2,i,k] <= 112.
All inputs are finite; a program needn't handle non-finite values.
Results may differ from the reference program's by a relative error of at most 0.0041.
Values may be sent and summed in bfloat16 or wider, within the bound.
No kernel may reach another device: no remote copies, remote signals or barrier semaphores. Data moves between devices by JAX's collectives and lax.ppermute only.
A program may use at most 128 MiB of HBM per device.

```python
from functools import partial
import jax
import jax.numpy as jnp
from jax import lax

B = 128
K = 16
H = 8
R = 32
PL = 16
GY = 128
GZ = 128
TX = 16
TY = 16
TZ = 16
NBR = 256
NXG = 128


def draw_pattern(key, part):
    key = jax.random.fold_in(key, 11)
    width = 2 * H + 1
    scores = jax.random.randint(key, (NBR, width), 0, 2 ** 20) * width + jnp.arange(width, dtype=jnp.int32)[None, :]
    order = jnp.argsort(scores, axis=1)[:, :K]
    offsets = jnp.arange(width, dtype=jnp.int32) - H
    chosen = offsets[order]
    return ((jnp.arange(NBR, dtype=jnp.int32)[:, None] + chosen) % NBR).astype(jnp.int32)


def draw_anchors(key, part):
    key = jax.random.fold_in(key, 23)
    key_x, key_y, key_z = jax.random.split(key, 3)
    margin = TX // 2
    shifts = jax.random.randint(key_x, (NBR, K), 0, PL + 1)
    shifts = shifts.at[0, 0].set(0).at[0, 1].set(margin).at[0, 2].set(margin - 1)
    groups = jnp.arange(NBR, dtype=jnp.int32) // R
    first = (groups[:, None] * PL - margin + shifts) % NXG
    second = jax.random.randint(key_y, (NBR, K), 0, GY - TY + 1)
    second = second.at[0, 0].set(0).at[0, 1].set(GY - TY)
    third = jax.random.randint(key_z, (NBR, K), 0, GZ - TZ + 1)
    third = third.at[0, 0].set(0).at[0, 1].set(GZ - TZ)
    return jnp.stack([first, second, third]).astype(jnp.int32)


def levels(own_key, dims, pieces, smallest, top_value):
    def one(dim, shards_of):
        heights = jax.random.uniform(jax.random.fold_in(jax.random.fold_in(own_key, 6), dim), (shards_of,), jnp.float32, smallest / len(pieces), top_value / len(pieces))
        return jnp.repeat(jnp.exp(heights), dims[dim] // shards_of).reshape((-1,) + (1,) * (len(dims) - dim - 1))

    loudness = one(*pieces[0])
    for cut in pieces[1:]:
        loudness = loudness * one(*cut)
    return loudness


def noise(rng, dims, scale, limit, cuts=(), kind=jnp.bfloat16):
    values = jax.random.normal(rng, dims, jnp.float32) * scale
    if len(cuts) > 0:
        values = levels(rng, dims, cuts, -0.22, 0.18) * values
    return jnp.clip(values, min=-limit, max=limit).astype(kind)


def setup_inputs(seed: int = 0) -> dict:
    key_of = jax.random.split(jax.random.key(seed), 6)
    return {
        "blocks": noise(key_of[0], (NBR, K, B, B), 0.15, 0.8984375, ((0, 8), (1, 4))),
        "pattern": draw_pattern(jax.random.fold_in(key_of[5], 71), 0),
        "anchors": draw_anchors(jax.random.fold_in(key_of[5], 71), 0),
        "basis_x": noise(key_of[3], (TX, B), B ** -0.5, 0.5),
        "basis_yz": noise(key_of[4], (B, TY * TZ), B ** -0.5, 0.5),
    }


def row_square(blocks, pattern, row_id):
    columns = pattern[row_id]
    gathered = blocks[columns].astype(jnp.float32)
    far_pattern = pattern[columns]
    matches = (far_pattern[:, :, None] == columns[None, None, :]).astype(jnp.float32)
    selected = jnp.einsum('kts,ktmn->ksmn', matches, gathered)
    return jnp.einsum('kmn,ksnp->smp', blocks[row_id].astype(jnp.float32), selected)


def reference(blocks, pattern, anchors, basis_x, basis_yz):
    square = lax.map(partial(row_square, blocks, pattern), jnp.arange(NBR, dtype=jnp.int32))
    density = square.astype(jnp.bfloat16)

    def place(canvas, inputs):
        row_density, row_anchor = inputs
        halves = jnp.einsum('am,kmn->kan', basis_x.astype(jnp.float32), row_density.astype(jnp.float32)).astype(jnp.bfloat16)
        halves = lax.optimization_barrier(halves)
        tile_values = jnp.einsum('kan,nc->kac', halves.astype(jnp.float32), basis_yz.astype(jnp.float32)).reshape(K, TX, TY, TZ)

        def add_one(slot, canvas_now):
            start = (row_anchor[0, slot].astype(jnp.int32), row_anchor[1, slot].astype(jnp.int32), row_anchor[2, slot].astype(jnp.int32))
            current = lax.dynamic_slice(canvas_now, start, (TX, TY, TZ))
            return lax.dynamic_update_slice(canvas_now, current + tile_values[slot], start)

        return lax.fori_loop(0, K, add_one, canvas), None

    canvas_start = jnp.zeros((NXG + TX, GY, GZ), jnp.float32)
    canvas, _ = lax.scan(place, canvas_start, (density, jnp.transpose(anchors, (1, 0, 2))))
    grid_values = canvas[:NXG].at[:TX].add(canvas[NXG:])
    return square, grid_values
```

```python
import functools

import jax
import jax.numpy as jnp
from jax import lax
from jax.experimental import pallas as pl
from jax.experimental.pallas import tpu as pltpu
from jax.sharding import PartitionSpec as P

H = 8
PL = 16
TX = 16
TY = 16
TZ = 16
CHUNK = H
LANES = 128


def across(value, axis, flip):
    peers = lax.axis_size(axis)
    return lax.ppermute(value, axis, [(i, i ^ flip) for i in range(peers)])


def from_behind(value, axis, by):
    peers = lax.axis_size(axis)
    return lax.ppermute(value, axis, [(i, (i + by) % peers) for i in range(peers)])


def between_chips(value, axis):
    peers = lax.axis_size(axis)
    return lax.ppermute(value, axis, [(i, (i + (1 if i % 2 else -1)) % peers) for i in range(peers)])


def after(value, *others):
    return lax.optimization_barrier((value,) + others)[0] if others else value


class Links:
    def __init__(self):
        self.sent = {}

    def send(self, link, value, depth, move):
        sent = self.sent.setdefault(link, [])
        if len(sent) >= depth:
            value = after(value, sent[-depth])
        sent.append(move(value))
        return sent[-1]


def second_hops(firsts, slots, axis, befores):
    peers = lax.axis_size(axis)
    bits = [1 << b for b in range(peers.bit_length() - 1)]
    shares = []
    if len(bits) == 2:
        for come, go, part in ((bits[0], bits[1], 0), (bits[1], bits[0], 1)):
            for first, count, hops in firsts:
                if len(firsts) == 1:
                    first, count = first + part * count // 2, count // 2
                    value = hops[come][first * slots : (first + count) * slots]
                elif (first > 0) == part:
                    value = hops[come]
                else:
                    continue
                value = across(after(value, *befores), axis, go)
                shares.append((come ^ go, first, count, value))
        return shares
    for first, count, hops in firsts:
        held = dict(hops)
        for place, bit in enumerate(bits):
            for distance in sorted(held):
                if distance & bit == 0 and distance >> (place + 1) == 0:
                    held[distance | bit] = across(held[distance], axis, bit)
                    shares.append((distance | bit, first, count, held[distance | bit]))
    return shares


def by_spot(chunk, chunks, core):
    return jnp.where(core == 0, chunk, chunks - 1 - chunk)


def in_spots(values, core):
    chunks = values.reshape((values.shape[0] // CHUNK, CHUNK) + values.shape[1:])
    return jnp.where(core == 0, chunks, chunks[::-1]).reshape(values.shape)


def slot_lookup(pattern, first_row, rows, total_rows, col_place, col_count, slots, core):
    kslots = pattern.shape[1]
    shares = jnp.arange(col_count, dtype=jnp.int32) ^ col_place
    picks = (jnp.arange(col_count, dtype=jnp.int32)[None, :] == shares[:, None]).astype(jnp.int32)
    offsets = (pattern - jnp.arange(total_rows, dtype=jnp.int32)[:, None] + H) % total_rows
    offsets = jnp.concatenate([offsets[total_rows - H :], offsets, offsets[:H]], axis=0)
    offsets = lax.dynamic_slice_in_dim(offsets, first_row, rows + 2 * H, 0)
    by_share = offsets.reshape(rows + 2 * H, 1, col_count, slots)
    offsets = jnp.sum(by_share * picks[None, :, :, None], axis=2).reshape(rows + 2 * H, kslots)
    own = offsets[H : H + rows]
    far = jnp.zeros((rows, kslots, kslots), jnp.int32)
    for w in range(2 * H + 1):
        far = far + jnp.where(own[:, :, None] == w, offsets[w : w + rows][:, None, :], 0)
    wanted = own[:, None, :slots] - own[:, :, None] + H
    matches = (far[:, :, None, :] == wanted[:, :, :, None]).astype(jnp.int32)
    matched = jnp.sum(matches, axis=3)
    slot = jnp.sum(matches * jnp.arange(kslots, dtype=jnp.int32), axis=3)
    line = jnp.arange(rows, dtype=jnp.int32)[:, None] + own
    spot = by_spot(line // CHUNK, rows // CHUNK + 2, core)
    place = (
        (spot[:, :, None] * col_count + slot // slots) * CHUNK + (line % CHUNK)[:, :, None]
    ) * slots + slot % slots
    return jnp.where(matched > 0, place, -1)


def square_kernel(
    first_spot, spots, sources, count, last, col_count, slots, kslots, core, look, planes, lines, turns, blocks, *refs
):
    pieces = refs[:count]
    refs = refs[count:]
    basis_x, basis_yz, slab_in, _, square = refs[:5]
    if last:
        middle, low, high, slab = refs[5:9]
        refs = refs[9:]
    else:
        slab = refs[5]
        refs = refs[6:]
    held, result, tiles, load_sems, store_sems = refs
    span = CHUNK * slots
    bsize = held.shape[-1]
    rows = spots * CHUNK
    spare = first_spot - 1
    all_spots = blocks.shape[0] // span

    def load(index):
        piece, take, share, spot_0, spot_1, first, count = sources[index]
        spot = spot_0 if spot_0 == spot_1 else jnp.where(core[0] == 0, spot_0, spot_1)
        to = held.at[pl.ds((((spot - spare) * col_count + share) * CHUNK + first) * slots, count * slots)]
        if piece is None:
            chunk = jnp.where(core[0] == 0, spot - 1, all_spots - spot)
            come = blocks.at[pl.ds((chunk * CHUNK + take) * slots, count * slots)]
        else:
            come = pieces[piece].at[pl.ds(take * slots, count * slots)]
        return pltpu.make_async_copy(come, to, load_sems.at[index])

    for index in range(len(sources)):
        load(index).start()
    if slab_in is None:
        slab[...] = jnp.zeros_like(slab)
    else:
        slab[...] = slab_in[...]
    tiles[...] = jnp.zeros_like(tiles)
    held[(spots + 2) * col_count * span] = jnp.zeros((bsize, bsize), held.dtype)
    lane = lax.broadcasted_iota(jnp.int32, (2 * PL, LANES), 1)

    def wait_for(spot):
        for index in range(len(sources)):
            if min(sources[index][3:5]) == spot:
                load(index).wait()

    for spot in range(2):
        wait_for(spare + spot)

    def place_tiles(row, spot):
        for s in range(slots):
            task = ((first_spot - 1) * CHUNK + row) * slots + s
            turn = turns[task]
            first = lines[task]
            group = ((lane + (LANES - turn)) & (LANES - 1)) // TZ
            halves = [
                pltpu.roll(
                    tiles[spot, s * 2 * PL : (s + 1) * 2 * PL, h * LANES : (h + 1) * LANES], turn, 1
                )
                for h in range(TY * TZ // LANES)
            ]
            per = LANES // TZ
            for b in range(TY):
                slab[first + b] = slab[first + b] + jnp.where(group == b % per, halves[b // per], 0.0)

    def out_copy(row):
        spot = first_spot - 1 + row // CHUNK
        chunk = jnp.where(core[0] == 0, spot, all_spots - 1 - spot)
        return pltpu.make_async_copy(
            result.at[row], square.at[chunk * CHUNK + row % CHUNK], store_sems.at[row]
        )

    def one_row(row, carry):
        for n in range(spots):

            @pl.when(row == n * CHUNK)
            def _():
                wait_for(spare + n + 2)

        spot = row % 2
        own_first = ((row // CHUNK + 1) * col_count) * span + (row % CHUNK) * slots
        overall = (first_spot - 1) * CHUNK + row

        def left(k):
            return held[own_first + (k // slots) * span + k % slots]

        def right(k, s):
            return held[look[(overall * slots + s) * kslots + k]]

        blocks_out = []
        lhs = jnp.concatenate([left(k) for k in range(kslots)], axis=1)
        for p in range(0, slots, 2):
            rhs = jnp.concatenate(
                [
                    jnp.concatenate([right(k, p), right(k, p + 1)], axis=1)
                    for k in range(kslots)
                ],
                axis=0,
            )
            total = jnp.dot(lhs, rhs, preferred_element_type=jnp.float32)
            blocks_out += [total[:, :bsize], total[:, bsize:]]
        for s in range(slots):
            result[row, s] = blocks_out[s]
        density = jnp.concatenate([block.astype(jnp.bfloat16) for block in blocks_out], axis=1)
        halves = jnp.dot(basis_x[...], density, preferred_element_type=jnp.float32)
        halves = jnp.concatenate([halves, jnp.zeros((2 * PL - TX, slots * bsize), jnp.float32)], axis=0)
        halves = [
            pltpu.roll(
                halves[:, s * bsize : (s + 1) * bsize], planes[overall * slots + s], 0
            ).astype(jnp.bfloat16)
            for s in range(slots)
        ]
        place_tiles(jnp.maximum(row - 1, 0), 1 - spot)
        tiles[spot] = jnp.dot(
            jnp.concatenate(halves, axis=0), basis_yz[...], preferred_element_type=jnp.float32
        )
        out_copy(row).start()
        return carry

    lax.fori_loop(0, rows, one_row, 0)
    place_tiles(rows - 1, (rows - 1) % 2)
    per = LANES // TZ

    def straighten(first, carry):
        edges = []
        for b in range(per):
            y = first * per + b
            line = pltpu.roll(slab[y], LANES - TZ * b, 1) if b else slab[y]
            middle[y] = line[TX // 2 : TX // 2 + PL]
            edges.append((line[: TX // 2], line[TX // 2 + PL :]))
        for b in range(0, per, 2):
            pair = (first * per + b) // 2
            for out, side in ((low, 0), (high, 1)):
                both = jnp.concatenate([edges[b][side], edges[b + 1][side]], axis=0)
                out[pair] = both.astype(out.dtype)
        return carry

    if last:
        lax.fori_loop(0, slab.shape[0] // per, straighten, 0)

    def finish(row, carry):
        out_copy(row).wait()
        return carry

    lax.fori_loop(0, rows, finish, 0)


def square_rows(first_spot, spots, sources, pieces, tables, blocks, bases, carried, last, slots, kslots, col_count):
    rows_all = blocks.shape[0] // slots
    bsize = blocks.shape[-1]
    smem = pl.BlockSpec(memory_space=pltpu.SMEM)
    vmem = pl.BlockSpec(memory_space=pltpu.VMEM)
    anywhere = pl.BlockSpec(memory_space=pl.ANY)
    square_shape = jax.ShapeDtypeStruct((rows_all, slots, bsize, bsize), jnp.float32)
    slab_shape = jax.ShapeDtypeStruct((LANES, 2 * PL, LANES), jnp.float32)
    body = functools.partial(square_kernel, first_spot, spots, sources, len(pieces), last, col_count, slots, kslots)
    inputs = tables + [blocks] + pieces + bases
    specs = [smem] * len(tables) + [anywhere] * (1 + len(pieces)) + [vmem] * len(bases)
    aliases = {}
    if carried is None:

        def kernel(*refs):
            body(*refs[: len(inputs)], None, None, *refs[len(inputs) :])

    else:
        kernel = body
        aliases = {len(inputs) + 1: 0}
        inputs = inputs + [carried[1], carried[0]]
        specs = specs + [vmem, anywhere]
    out_shape, slab = (square_shape, slab_shape), []
    if last:
        rim_shape = jax.ShapeDtypeStruct((LANES // 2, TX, LANES), jnp.bfloat16)
        middle_shape = jax.ShapeDtypeStruct((LANES, PL, LANES), jnp.float32)
        out_shape = (square_shape, middle_shape, rim_shape, rim_shape)
        slab = [pltpu.VMEM(slab_shape.shape, jnp.float32)]
    return pl.pallas_call(
        kernel,
        out_shape=out_shape,
        in_specs=specs,
        out_specs=(anywhere,) + (vmem,) * (len(out_shape) - 1),
        scratch_shapes=slab
        + [
            pltpu.VMEM(((spots + 2) * CHUNK * kslots + 1, bsize, bsize), jnp.bfloat16),
            pltpu.VMEM((spots * CHUNK, slots, bsize, bsize), jnp.float32),
            pltpu.VMEM((2, slots * 2 * PL, TY * TZ), jnp.float32),
            pltpu.SemaphoreType.DMA((len(sources),)),
            pltpu.SemaphoreType.DMA((spots * CHUNK,)),
        ],
        input_output_aliases=aliases,
        compiler_params=pltpu.CompilerParams(vmem_limit_bytes=56 * 1024 * 1024),
        cost_estimate=pl.CostEstimate(
            flops=6 * spots * CHUNK * slots * kslots * bsize**3,
            bytes_accessed=24 * 1024 * 1024,
            transcendentals=0,
        ),
        name="square_and_place",
    )(*inputs)


def per_device(blocks, pattern, anchors, basis_x, basis_yz):
    rows, slots, bsize, _ = blocks.shape
    kslots = pattern.shape[1]
    row_count = lax.axis_size("row")
    col_count = lax.axis_size("col")
    row_place = lax.axis_index("row")
    col_place = lax.axis_index("col")
    core = row_place % 2
    total_rows = rows * row_count
    first_row = row_place * rows
    spots = rows // CHUNK
    flat = blocks.reshape(rows * slots, bsize, bsize)

    def own(spot, first, count):
        chunk = by_spot(spot, spots + 2, core) - 1
        return lax.dynamic_slice_in_dim(flat, (chunk * CHUNK + first) * slots, count * slots, 0)

    links = Links()
    moves = {
        "between": functools.partial(between_chips, axis="row"),
        "inside": functools.partial(across, axis="row", flip=1),
    }
    outer = own(1, 0, CHUNK)
    middle = [flat[n * CHUNK * slots : (n + 1) * CHUNK * slots] for n in range(1, spots - 1)]
    inner = own(spots, 0, CHUNK)
    loads = [(None, 0, 0, spot, spot, 0, CHUNK) for spot in range(1, spots + 1)]
    pieces = []

    def keep(value, take, share, spot_0, spot_1, first, count):
        if not any(value is piece for piece in pieces):
            pieces.append(value)
        index = [value is piece for piece in pieces].index(True)
        loads.append((index, take, share, spot_0, spot_1, first, count))

    bits = [1 << b for b in range(col_count.bit_length() - 1)]

    def hop(parts, befores=(), turns=None):
        hops = [{} for _ in parts]
        for place, bit in enumerate(bits):
            for n in range(len(parts)):
                if turns is None or (n == (place % 2) * (len(parts) - 1)) == turns:
                    hops[n][bit] = across(after(parts[n], *befores), "col", bit)
        return hops

    def shares_of(parts, hops, count, befores=()):
        firsts = [(n * count, count, got) for n, got in enumerate(hops)]
        later = second_hops(firsts, slots, "col", befores)
        shares = [(bit, first, count, got[bit]) for first, count, got in firsts for bit in bits]
        return shares + later, [share[3] for share in later]

    outer_hops = hop([outer])
    shares, done = shares_of([outer], outer_hops, CHUNK)
    over = moves["between"](outer)
    keep(over, 0, 0, 0, 0, 0, CHUNK)
    over = moves["between"](after(jnp.concatenate([share[3] for share in shares], axis=0), over))
    take = 0
    for distance, first, count, value in shares:
        keep(value, 0, distance, 1, 1, first, count)
        keep(over, take, distance, 0, 0, first, count)
        take += count
    leading = hop(middle, done, turns=True)
    trailing = hop(middle, done, turns=False)
    middle_hops = [{**one, **other} for one, other in zip(leading, trailing)]
    shares, done = shares_of(middle, middle_hops, CHUNK)
    for distance, first, count, value in shares:
        chunk = first // CHUNK + 2
        keep(value, 0, distance, chunk, spots + 1 - chunk, 0, CHUNK)
    done = done + [value for one in trailing for value in one.values()]
    inner_hops = hop([inner], done)

    def rows_from(first_spot, carried):
        fits = range(first_spot - 1, first_spot + spots // 2 + 1)
        chosen = [load for load in loads if load[3] in fits and load[4] in fits]
        chosen.sort(key=lambda load: min(load[3:5]))
        used = sorted({load[0] for load in chosen if load[0] is not None})
        sources = [
            (None if load[0] is None else used.index(load[0]),) + load[1:] for load in chosen
        ]
        return square_rows(
            first_spot,
            spots // 2,
            sources,
            [pieces[index] for index in used],
            tables,
            flat,
            bases,
            carried,
            first_spot > 1,
            slots,
            kslots,
            col_count,
        )

    look = slot_lookup(pattern, first_row, rows, total_rows, col_place, col_count, slots, core)
    look = in_spots(jnp.transpose(look, (0, 2, 1)), core).reshape(2, -1)
    span = CHUNK * kslots
    skipped = jnp.arange(2, dtype=jnp.int32)[:, None] * (spots // 2 * span)
    look = jnp.where(look < 0, (spots // 2 + 2) * span, look - skipped).reshape(-1)
    own_anchors = lax.dynamic_slice(anchors, (0, first_row, col_place * slots), (3, rows, slots))
    own_anchors = in_spots(jnp.transpose(own_anchors, (1, 0, 2)), core)
    own_anchors = jnp.transpose(own_anchors, (1, 0, 2)).reshape(3, rows * slots)
    margin = TX // 2
    planes = (own_anchors[0] - row_place * PL + margin) % (PL * row_count)
    lines = own_anchors[1]
    turns = (own_anchors[2] + TZ * own_anchors[1]) % LANES
    tables = [jnp.reshape(core, (1,)), look, planes, lines, turns]
    bases = [basis_x, basis_yz]

    early = rows_from(1, None)
    shares, _ = shares_of([inner], inner_hops, CHUNK, early[1:2])
    for distance, first, count, value in shares:
        keep(value, 0, distance, spots, spots, first, count)
    for distance, first, count, value in [(0, 0, CHUNK, inner)] + shares:
        if distance.bit_count() < 2:
            value = after(value, early[1])
        come = links.send("inside", value, 2, moves["inside"])
        keep(come, 0, distance, spots + 1, spots + 1, first, count)
    square, middle_planes, low, high = rows_from(1 + spots // 2, early)

    wire = jnp.bfloat16
    rims = [from_behind(high, "row", 1), from_behind(low, "row", -1)]
    rims = [rim.reshape(LANES, margin, LANES) for rim in rims]
    folded = middle_planes + jnp.concatenate(rims, axis=1).astype(jnp.float32)
    share = LANES // col_count
    by_share = folded.reshape(col_count, share, PL, LANES)
    total = lax.dynamic_index_in_dim(by_share, col_place, 0, keepdims=False)
    for distance in range(1, col_count):
        sent = lax.dynamic_index_in_dim(by_share, col_place ^ distance, 0, keepdims=False)
        total = total + across(sent.astype(wire), "col", distance).astype(jnp.float32)
    return square, jnp.transpose(total, (1, 0, 2))


def solution(mesh):
    placed = (P("row", "col", None, None), P(), P(), P(), P())
    return jax.shard_map(
        per_device,
        mesh=mesh,
        in_specs=placed,
        out_specs=(P("row", "col", None, None), P("row", "col", None)),
        check_vma=False,
    )
```

```python
import functools

import jax
import jax.numpy as jnp
from jax import lax
from jax.experimental import pallas as pl
from jax.experimental.pallas import tpu as pltpu
from jax.sharding import PartitionSpec as P

H = 8
PL = 16
TX = 16
TY = 16
TZ = 16
CHUNK = H
ROWS = 4
LANES = 128


def across(value, axis, flip):
    peers = lax.axis_size(axis)
    return lax.ppermute(value, axis, [(i, i ^ flip) for i in range(peers)])


def from_behind(value, axis, by):
    peers = lax.axis_size(axis)
    return lax.ppermute(value, axis, [(i, (i + by) % peers) for i in range(peers)])


def between_chips(value, axis):
    peers = lax.axis_size(axis)
    return lax.ppermute(value, axis, [(i, (i + (1 if i % 2 else -1)) % peers) for i in range(peers)])


def after(value, *others):
    return lax.optimization_barrier((value,) + others)[0] if others else value


def second_hops(firsts, slots, axis, befores, cut=None):
    peers = lax.axis_size(axis)
    bits = [1 << b for b in range(peers.bit_length() - 1)]
    shares = []
    if len(bits) == 2:
        for come, go, part in ((bits[0], bits[1], 0), (bits[1], bits[0], 1)):
            for first, count, hops in firsts:
                if len(firsts) == 1:
                    first, count = first + part * count // 2, count // 2
                    value = hops[come][first * slots : (first + count) * slots]
                elif (first > 0) == part:
                    value = hops[come]
                else:
                    continue
                for take in range(0, count, cut or count):
                    some = value[take * slots : (take + (cut or count)) * slots]
                    some = across(after(some, *befores), axis, go)
                    shares.append((come ^ go, first + take, cut or count, some))
        return shares
    for first, count, hops in firsts:
        held = dict(hops)
        for place, bit in enumerate(bits):
            for distance in sorted(held):
                if distance & bit == 0 and distance >> (place + 1) == 0:
                    held[distance | bit] = across(held[distance], axis, bit)
                    shares.append((distance | bit, first, count, held[distance | bit]))
    return shares


def by_spot(chunk, chunks, core):
    return jnp.where(core == 0, chunk, chunks - 1 - chunk)


def in_spots(values, core):
    chunks = values.reshape((values.shape[0] // CHUNK, CHUNK) + values.shape[1:])
    return jnp.where(core == 0, chunks, chunks[::-1]).reshape(values.shape)


def slot_lookup(pattern, first_row, rows, total_rows, col_place, col_count, slots, core):
    kslots = pattern.shape[1]
    shares = jnp.arange(col_count, dtype=jnp.int32) ^ col_place
    picks = (jnp.arange(col_count, dtype=jnp.int32)[None, :] == shares[:, None]).astype(jnp.int32)
    offsets = (pattern - jnp.arange(total_rows, dtype=jnp.int32)[:, None] + H) % total_rows
    offsets = jnp.concatenate([offsets[total_rows - H :], offsets, offsets[:H]], axis=0)
    offsets = lax.dynamic_slice_in_dim(offsets, first_row, rows + 2 * H, 0)
    by_share = offsets.reshape(rows + 2 * H, 1, col_count, slots)
    offsets = jnp.sum(by_share * picks[None, :, :, None], axis=2).reshape(rows + 2 * H, kslots)
    own = offsets[H : H + rows]
    far = jnp.zeros((rows, kslots, kslots), jnp.int32)
    for w in range(2 * H + 1):
        far = far + jnp.where(own[:, :, None] == w, offsets[w : w + rows][:, None, :], 0)
    wanted = own[:, None, :slots] - own[:, :, None] + H
    matches = (far[:, :, None, :] == wanted[:, :, :, None]).astype(jnp.int32)
    matched = jnp.sum(matches, axis=3)
    slot = jnp.sum(matches * jnp.arange(kslots, dtype=jnp.int32), axis=3)
    line = jnp.arange(rows, dtype=jnp.int32)[:, None] + own
    spot = by_spot(line // CHUNK, rows // CHUNK + 2, core)
    place = (
        (spot[:, :, None] * col_count + slot // slots) * CHUNK + (line % CHUNK)[:, :, None]
    ) * slots + slot % slots
    return jnp.where(matched > 0, place, -1)


def square_kernel(
    first_spot, spots, sources, count, last, col_count, slots, kslots, core, look, planes, lines, turns, blocks, *refs
):
    pieces = refs[:count]
    refs = refs[count:]
    basis_x, basis_yz, slab_in, _, square = refs[:5]
    if last:
        middle, low, high, slab, before, before_sem = refs[5:11]
        refs = refs[11:]
    else:
        slab = refs[5]
        refs = refs[6:]
    held, result, density, tiles, load_sems, store_sems = refs
    span = CHUNK * slots
    bsize = held.shape[-1]
    rows = spots * CHUNK
    spare = first_spot - 1
    all_spots = blocks.shape[0] // span

    def load(index, which=0):
        piece, take, share, spot_0, spot_1, first, count = sources[index]
        spot = spot_0 if spot_0 == spot_1 else jnp.where(core[0] == 0, spot_0, spot_1)
        to = held.at[pl.ds((((spot - spare) * col_count + share) * CHUNK + first) * slots, count * slots)]
        if piece is None:
            chunk = jnp.where(core[0] == 0, spot - 1, all_spots - spot)
            come = blocks.at[pl.ds((chunk * CHUNK + take) * slots, count * slots)]
        else:
            if isinstance(piece, tuple):
                piece, take = piece[which], take[which]
            come = pieces[piece].at[pl.ds(take * slots, count * slots)]
        return pltpu.make_async_copy(come, to, load_sems.at[index])

    def start(index, which):
        @pl.when(core[0] == which)
        def _():
            load(index, which).start()

    for index in range(len(sources)):
        if isinstance(sources[index][0], tuple):
            for which in range(2):
                start(index, which)
        else:
            load(index).start()
    if last:
        earlier = pltpu.make_async_copy(slab_in, before, before_sem)
        earlier.start()
    if last or slab_in is None:
        slab[...] = jnp.zeros_like(slab)
    else:
        slab[...] = slab_in[...]
    tiles[...] = jnp.zeros_like(tiles)
    density[...] = jnp.zeros_like(density)
    held[(spots + 2) * col_count * span] = jnp.zeros((bsize, bsize), held.dtype)
    lane = lax.broadcasted_iota(jnp.int32, (2 * PL, LANES), 1)

    def wait_for(spot):
        for index in range(len(sources)):
            if min(sources[index][3:5]) == spot:
                load(index).wait()

    for spot in range(2):
        wait_for(spare + spot)

    per = LANES // TZ

    def place(row, turn_of):
        row = jnp.maximum(row, 0)
        for s in range(slots):
            task = ((first_spot - 1) * CHUNK + row) * slots + s
            turn = turns[task]
            first = lines[task]
            group = ((lane + (LANES - turn)) & (LANES - 1)) // TZ
            halves = [
                pltpu.roll(
                    tiles[turn_of, s * 2 * PL : (s + 1) * 2 * PL, h * LANES : (h + 1) * LANES], turn, 1
                )
                for h in range(TY * TZ // LANES)
            ]
            for b in range(TY):
                slab[first + b] = slab[first + b] + jnp.where(group == b % per, halves[b // per], 0.0)

    def spread(row, turn_of):
        overall = (first_spot - 1) * CHUNK + jnp.maximum(row, 0)
        halves = jnp.dot(basis_x[...], density[turn_of], preferred_element_type=jnp.float32)
        halves = jnp.concatenate([halves, jnp.zeros((2 * PL - TX, slots * bsize), jnp.float32)], axis=0)
        halves = [
            pltpu.roll(
                halves[:, s * bsize : (s + 1) * bsize], planes[overall * slots + s], 0
            ).astype(jnp.bfloat16)
            for s in range(slots)
        ]
        tiles[turn_of] = jnp.dot(
            jnp.concatenate(halves, axis=0), basis_yz[...], preferred_element_type=jnp.float32
        )

    def out_copy(row):
        spot = first_spot - 1 + row // CHUNK
        chunk = jnp.where(core[0] == 0, spot, all_spots - 1 - spot)
        return pltpu.make_async_copy(
            result.at[row], square.at[chunk * CHUNK + row % CHUNK], store_sems.at[row]
        )

    def product(row, turn_of):
        own_first = ((row // CHUNK + 1) * col_count) * span + (row % CHUNK) * slots
        overall = (first_spot - 1) * CHUNK + row

        def left(k):
            return held[own_first + (k // slots) * span + k % slots]

        def right(k, s):
            return held[look[(overall * slots + s) * kslots + k]]

        lhs = jnp.concatenate([left(k) for k in range(kslots)], axis=1)
        rhs = jnp.concatenate(
            [
                jnp.concatenate([right(k, s) for s in range(slots)], axis=1)
                for k in range(kslots)
            ],
            axis=0,
        )
        total = jnp.dot(lhs, rhs, preferred_element_type=jnp.float32)
        for s in range(slots):
            result[row, s] = total[:, s * bsize : (s + 1) * bsize]
        density[turn_of] = total.astype(density.dtype)
        out_copy(row).start()

    steps = CHUNK // ROWS

    def some_rows(step, carry):
        for n in range(spots):

            @pl.when(step == n * steps)
            def _():
                wait_for(spare + 2 + n)

        for r in range(ROWS):
            row = step * ROWS + r
            place(row - 2, r % 2)
            spread(row - 1, 1 - r % 2)
            product(row, r % 2)
        return carry

    lax.fori_loop(0, rows // ROWS, some_rows, 0)
    place(rows - 2, 0)
    spread(rows - 1, 1)
    place(rows - 1, 1)

    def straighten(first, carry):
        edges = []
        for b in range(per):
            y = first * per + b
            line = slab[y] + before[y]
            line = pltpu.roll(line, LANES - TZ * b, 1) if b else line
            middle[y] = line[TX // 2 : TX // 2 + PL]
            edges.append((line[: TX // 2], line[TX // 2 + PL :]))
        for b in range(0, per, 2):
            pair = (first * per + b) // 2
            for out, side in ((low, 0), (high, 1)):
                both = jnp.concatenate([edges[b][side], edges[b + 1][side]], axis=0)
                out[pair] = both.astype(out.dtype)
        return carry

    if last:
        earlier.wait()
        lax.fori_loop(0, slab.shape[0] // per, straighten, 0)

    def finish(row, carry):
        out_copy(row).wait()
        return carry

    lax.fori_loop(0, rows, finish, 0)


def square_rows(first_spot, spots, sources, pieces, tables, blocks, bases, carried, last, slots, kslots, col_count):
    rows_all = blocks.shape[0] // slots
    bsize = blocks.shape[-1]
    smem = pl.BlockSpec(memory_space=pltpu.SMEM)
    vmem = pl.BlockSpec(memory_space=pltpu.VMEM)
    anywhere = pl.BlockSpec(memory_space=pl.ANY)
    square_shape = jax.ShapeDtypeStruct((rows_all, slots, bsize, bsize), jnp.float32)
    slab_shape = jax.ShapeDtypeStruct((LANES, 2 * PL, LANES), jnp.float32)
    body = functools.partial(square_kernel, first_spot, spots, sources, len(pieces), last, col_count, slots, kslots)
    inputs = tables + [blocks] + pieces + bases
    specs = [smem] * len(tables) + [anywhere] * (1 + len(pieces)) + [vmem] * len(bases)
    aliases = {}
    if carried is None:

        def kernel(*refs):
            body(*refs[: len(inputs)], None, None, *refs[len(inputs) :])

    else:
        kernel = body
        aliases = {len(inputs) + 1: 0}
        inputs = inputs + [carried[1], carried[0]]
        specs = specs + [anywhere if last else vmem, anywhere]
    out_shape, slab = (square_shape, slab_shape), []
    if last:
        rim_shape = jax.ShapeDtypeStruct((LANES // 2, TX, LANES), jnp.bfloat16)
        middle_shape = jax.ShapeDtypeStruct((LANES, PL, LANES), jnp.float32)
        out_shape = (square_shape, middle_shape, rim_shape, rim_shape)
        slab = [pltpu.VMEM(slab_shape.shape, jnp.float32)] * 2 + [pltpu.SemaphoreType.DMA]
    return pl.pallas_call(
        kernel,
        out_shape=out_shape,
        in_specs=specs,
        out_specs=(anywhere,) + (vmem,) * (len(out_shape) - 1),
        scratch_shapes=slab
        + [
            pltpu.VMEM(((spots + 2) * CHUNK * kslots + 1, bsize, bsize), jnp.bfloat16),
            pltpu.VMEM((spots * CHUNK, slots, bsize, bsize), jnp.float32),
            pltpu.VMEM((2, bsize, slots * bsize), jnp.bfloat16),
            pltpu.VMEM((2, slots * 2 * PL, TY * TZ), jnp.float32),
            pltpu.SemaphoreType.DMA((len(sources),)),
            pltpu.SemaphoreType.DMA((spots * CHUNK,)),
        ],
        input_output_aliases=aliases,
        compiler_params=pltpu.CompilerParams(vmem_limit_bytes=29 * 1024 * 1024),
        cost_estimate=pl.CostEstimate(
            flops=6 * spots * CHUNK * slots * kslots * bsize**3,
            bytes_accessed=24 * 1024 * 1024,
            transcendentals=0,
        ),
        name="square_and_place",
    )(*inputs)


def per_device(blocks, pattern, anchors, basis_x, basis_yz):
    rows, slots, bsize, _ = blocks.shape
    kslots = pattern.shape[1]
    row_count = lax.axis_size("row")
    col_count = lax.axis_size("col")
    row_place = lax.axis_index("row")
    col_place = lax.axis_index("col")
    core = row_place % 2
    total_rows = rows * row_count
    first_row = row_place * rows
    spots = rows // CHUNK
    flat = blocks.reshape(rows * slots, bsize, bsize)

    def own(spot, first, count, befores=()):
        chunk = by_spot(spot, spots + 2, core) - 1
        take = after((chunk * CHUNK + first) * slots, *befores)
        return lax.dynamic_slice_in_dim(flat, take, count * slots, 0)

    moves = {
        "between": functools.partial(between_chips, axis="row"),
        "inside": functools.partial(across, axis="row", flip=1),
    }
    edge = CHUNK * slots
    outer = jnp.where(core == 0, flat[:edge], flat[rows * slots - edge :])
    middle = [flat[n * CHUNK * slots : (n + 1) * CHUNK * slots] for n in range(1, spots - 1)]
    loads = [(None, 0, 0, spot, spot, 0, CHUNK) for spot in range(1, spots + 1)]
    pieces = []

    def keep(value, take, share, spot_0, spot_1, first, count):
        if not any(value is piece for piece in pieces):
            pieces.append(value)
        index = [value is piece for piece in pieces].index(True)
        loads.append((index, take, share, spot_0, spot_1, first, count))

    bits = [1 << b for b in range(col_count.bit_length() - 1)]

    def hop(parts, befores=(), turns=None):
        hops = [{} for _ in parts]
        for place, bit in enumerate(bits):
            for n in range(len(parts)):
                if turns is None or (n == (place % 2) * (len(parts) - 1)) == turns:
                    hops[n][bit] = across(after(parts[n], *befores), "col", bit)
        return hops

    def shares_of(parts, hops, count, befores=(), cut=None):
        firsts = [(n * count, count, got) for n, got in enumerate(hops)]
        later = second_hops(firsts, slots, "col", befores, cut)
        shares = [(bit, first, count, got[bit]) for first, count, got in firsts for bit in bits]
        return shares + later, [share[3] for share in later]

    outer_hops = hop([outer])
    shares, done = shares_of([outer], outer_hops, CHUNK)
    inner = own(spots, 0, CHUNK, done)
    over = moves["between"](outer)
    keep(over, 0, 0, 0, 0, 0, CHUNK)
    over = moves["between"](after(jnp.concatenate([share[3] for share in shares], axis=0), over))
    take = 0
    for distance, first, count, value in shares:
        keep(value, 0, distance, 1, 1, first, count)
        keep(over, take, distance, 0, 0, first, count)
        take += count
    leading = hop(middle, done, turns=True)
    trailing = hop(middle, done, turns=False)
    middle_hops = [{**one, **other} for one, other in zip(leading, trailing)]
    shares, _ = shares_of(middle, middle_hops, CHUNK, cut=CHUNK // 2)
    for distance, first, count, value in shares:
        chunk = first // CHUNK + 2
        keep(value, 0, distance, chunk, spots + 1 - chunk, first % CHUNK, count)
    done = [share[3] for share in shares if share[0].bit_count() > 1 and share[1] % CHUNK == 0]
    done = done + [value for one in trailing for value in one.values()]
    inner_hops = hop([inner], done)
    def rows_from(call, carried):
        first_spot, spot_count = call
        fits = range(first_spot - 1, first_spot + spot_count + 1)
        chosen = []
        for load in loads:
            if load[3] in fits and load[4] in fits:
                chosen.append(load)
            elif load[3] in fits:
                key = (load[2], load[3]) + load[5:]
                twin = [other for other in loads if (other[2], other[4]) + other[5:] == key]
                chosen.append(
                    ((load[0], twin[0][0]), (load[1], twin[0][1])) + (load[2], load[3], load[3]) + load[5:]
                )
        chosen.sort(key=lambda load: (min(load[3:5]), load[5]))
        used = set()
        for load in chosen:
            used.update(load[0] if isinstance(load[0], tuple) else (load[0],))
        used = sorted(used - {None})

        def place_of(piece):
            if isinstance(piece, tuple):
                return tuple(used.index(one) for one in piece)
            return None if piece is None else used.index(piece)

        sources = [(place_of(load[0]),) + load[1:] for load in chosen]
        return square_rows(
            first_spot,
            spot_count,
            sources,
            [pieces[index] for index in used],
            tables,
            flat,
            bases,
            carried,
            call == calls[-1],
            slots,
            kslots,
            col_count,
        )

    led = [value for one in leading for value in one.values()]
    pattern = after(pattern, *led)
    anchors = after(anchors, *led)
    look = slot_lookup(pattern, first_row, rows, total_rows, col_place, col_count, slots, core)
    look = in_spots(jnp.transpose(look, (0, 2, 1)), core).reshape(spots, -1)
    calls = [(2, spots // 2 - 1), (1, 1), (spots // 2 + 1, spots // 2)]
    span = CHUNK * kslots
    skipped, spare = [0] * spots, [0] * spots
    for first_spot, count in calls:
        for spot in range(first_spot, first_spot + count):
            skipped[spot - 1] = (first_spot - 1) * span
            spare[spot - 1] = (count + 2) * span
    skipped = jnp.array(skipped, jnp.int32)[:, None]
    spare = jnp.array(spare, jnp.int32)[:, None]
    look = jnp.where(look < 0, spare, look - skipped).reshape(-1)
    own_anchors = lax.dynamic_slice(anchors, (0, first_row, col_place * slots), (3, rows, slots))
    own_anchors = in_spots(jnp.transpose(own_anchors, (1, 0, 2)), core)
    own_anchors = jnp.transpose(own_anchors, (1, 0, 2)).reshape(3, rows * slots)
    margin = TX // 2
    planes = (own_anchors[0] - row_place * PL + margin) % (PL * row_count)
    lines = own_anchors[1]
    turns = (own_anchors[2] + TZ * own_anchors[1]) % LANES
    tables = [jnp.reshape(core, (1,)), look, planes, lines, turns]
    bases = [basis_x, basis_yz]

    early = rows_from(calls[0], None)
    shares, _ = shares_of([inner], inner_hops, CHUNK, early[1:2])
    halfway = rows_from(calls[1], early)
    for distance, first, count, value in shares:
        keep(value, 0, distance, spots, spots, first, count)
    for distance, first, count, value in [(0, 0, CHUNK, inner)] + shares:
        value = after(value, (early if distance.bit_count() < 2 else halfway)[1])
        come = moves["inside"](value)
        keep(come, 0, distance, spots + 1, spots + 1, first, count)
    square, middle_planes, low, high = rows_from(calls[2], halfway)

    wire = jnp.bfloat16
    rims = [from_behind(high, "row", 1), from_behind(low, "row", -1)]
    rims = [rim.reshape(LANES, margin, LANES) for rim in rims]
    folded = middle_planes + jnp.concatenate(rims, axis=1).astype(jnp.float32)
    share = LANES // col_count
    by_share = folded.reshape(col_count, share, PL, LANES)
    total = lax.dynamic_index_in_dim(by_share, col_place, 0, keepdims=False)
    for distance in sorted(range(1, col_count), key=lambda d: -d.bit_count()):
        sent = lax.dynamic_index_in_dim(by_share, col_place ^ distance, 0, keepdims=False)
        total = total + across(sent.astype(wire), "col", distance).astype(jnp.float32)
    return square, jnp.transpose(total, (1, 0, 2))


def solution(mesh):
    placed = (P("row", "col", None, None), P(), P(), P(), P())
    return jax.shard_map(
        per_device,
        mesh=mesh,
        in_specs=placed,
        out_specs=(P("row", "col", None, None), P("row", "col", None)),
        check_vma=False,
    )
```
